256 devices in a mesh: ctx: 64 (over x, z, core), dp: 4 (over y).
Axes of the slice: x: 4, y: 4, z: 8, core: 2. Of those that a mesh axis runs over, the one named last changes fastest.
Arguments:
- projected: bfloat16 [65536, 12288], P(('dp', 'ctx')), parts along dimension 0, may hold values from -6 to 6
- taps: float32 [7, 12288], replicated, may hold values from -2 to 2
- decays: float32 [4096, 16], replicated, may hold values from 3.0517578e-05 to 0.033
- residues: float32 [4096, 16], replicated, may hold values from -1.5 to 1.5
Outputs:
- mixed: float32 [65536, 4096], P(('dp', 'ctx')), parts along dimension 0
The draws below stay inside these ranges and needn't reach their ends.
There are 4 independent parts, one for each index of `dp`. The reference program is written for one: setup_inputs(seed, part) draws one part's arguments, and reference() takes and returns one part's arrays. A program takes and returns all parts, laid end to end along the dimension named above; an argument that names none is the same for every part. Nothing has to cross between parts.
All inputs are finite; a program needn't handle non-finite values.
Results may differ from the reference program's by a relative error of at most 0.0041.
Values may be sent and summed in bfloat16 or wider, within the bound.
A program may use at most 128 MiB of HBM per device.

```python
import math
import jax
import jax.numpy as jnp
from jax import lax

D = 4096
MODES = 16
KTAPS = 7
LENGTH = 16384


def block_scale(rng, extent, shards, smallest, top_value):
    gain = 1.0
    for position, blocks in shards:
        steps = jax.random.uniform(jax.random.fold_in(jax.random.fold_in(rng, 6), position), (blocks,), jnp.float32, smallest / len(shards), top_value / len(shards))
        gain = gain * jnp.repeat(jnp.exp(steps), extent[position] // blocks).reshape((-1,) + (1,) * (len(extent) - 1 - position))
    return gain


def centred(own_key, shape, deviation, limit, cuts=(), kind=jnp.bfloat16):
    entries = jax.random.normal(own_key, shape, jnp.float32) * deviation
    if len(cuts) > 0:
        entries = block_scale(own_key, shape, cuts, -0.22, 0.18) * entries
    return jnp.clip(entries, min=-limit, max=limit).astype(kind)


def setup_inputs(seed: int = 0, part: int = 0) -> dict:
    keys = jax.random.split(jax.random.key(seed), 5)
    part_keys = jax.random.split(jax.random.fold_in(keys[4], part), 5)
    projected = centred(part_keys[0], (LENGTH, 3 * D), 1.0, 6.0, ((0, 64),))
    taps = centred(keys[1], (KTAPS, 3 * D), KTAPS ** -0.5, 2.0, (), jnp.float32)
    decays = jnp.clip(jnp.exp(jax.random.uniform(keys[2], (D, MODES), jnp.float32, math.log(3.0517578125e-05), math.log(0.033))), 3.0517578125e-05, 0.033)
    residues = centred(keys[3], (D, MODES), 0.25, 1.5, (), jnp.float32)
    return {"projected": projected, "taps": taps, "decays": decays, "residues": residues}


def reference(projected, taps, decays, residues):
    lead = KTAPS - 1

    def short_part(part):
        column = projected[:, part * D:(part + 1) * D].astype(jnp.float32)
        padded = jnp.concatenate([jnp.zeros((lead, D), jnp.float32), column], 0)
        total = jnp.zeros((LENGTH, D), jnp.float32)
        for shift in range(KTAPS):
            total = total + taps[shift, part * D:(part + 1) * D][None, :] * padded[lead - shift:lead - shift + LENGTH]
        return total
    queries = short_part(0)
    gated = (short_part(1) * short_part(2)).astype(jnp.bfloat16)
    width = math.gcd(D, 64)
    blocks = D // width
    scale = residues * jnp.sqrt(-jnp.expm1(-2.0 * decays))
    times = jnp.arange(LENGTH).astype(jnp.float32)

    def convolve(items):
        field, rates, weights = items
        kernel = lax.optimization_barrier(jnp.sum(weights[None, :, :] * jnp.exp(-rates[None, :, :] * times[:, None, None]), axis=2))
        spectrum = jnp.fft.rfft(field.astype(jnp.float32), n=2 * LENGTH, axis=0) * jnp.fft.rfft(kernel, n=2 * LENGTH, axis=0)
        return jnp.fft.irfft(spectrum, n=2 * LENGTH, axis=0)[:LENGTH]
    fields = gated.reshape(LENGTH, blocks, width).transpose(1, 0, 2)
    result = lax.map(convolve, (fields, decays.reshape(blocks, width, MODES), scale.reshape(blocks, width, MODES)))
    long_field = result.transpose(1, 0, 2).reshape(LENGTH, D).astype(jnp.bfloat16)
    return queries * long_field.astype(jnp.float32)
```

```python
import jax
import jax.numpy as jnp
import ml_dtypes
import numpy as np
from jax import lax
from jax.sharding import PartitionSpec as P

NODES = 13


def chunk_basis(length):
    place = np.cos((np.arange(NODES) + 0.5) * np.pi / NODES)
    nodes = 0.5 * (length - 1) * (1.0 + place)
    token = np.arange(length)
    basis = np.ones((length, NODES))
    for j in range(NODES):
        for k in range(NODES):
            if k != j:
                basis[:, j] *= (token - nodes[k]) / (nodes[j] - nodes[k])
    return nodes, basis


def split_pair(table):
    high = table.astype(ml_dtypes.bfloat16)
    low = (table - high.astype(np.float64)).astype(ml_dtypes.bfloat16)
    return high, low


def short_filter(projected, taps):
    lead = taps.shape[0] - 1
    rows = projected.shape[0]
    peers = lax.axis_size("ctx")
    edge = lax.ppermute(projected[rows - lead :], "ctx", [(i, i + 1) for i in range(peers - 1)])
    joined = jnp.concatenate([edge, projected], 0)
    total = jnp.zeros(projected.shape, jnp.float32)
    for shift in range(taps.shape[0]):
        total = total + taps[shift][None, :] * joined[lead - shift : lead - shift + rows].astype(jnp.float32)
    return total


def mm(a, b):
    return jnp.dot(a, b, preferred_element_type=jnp.float32)


def shards(projected, taps, decays, residues):
    rows = projected.shape[0]
    width = taps.shape[1] // 3
    peers = lax.axis_size("ctx")
    own = width // peers
    nodes, basis = chunk_basis(rows)
    lag = np.arange(rows)[:, None] - np.arange(rows)[None, :]
    toeplitz = np.where(lag[None] >= 0, basis.T[:, np.maximum(lag, 0)], 0.0)
    node = jnp.asarray(nodes, jnp.float32)

    filtered = short_filter(projected, taps)
    queries = filtered[:, :width]
    gated = (filtered[:, width : 2 * width] * filtered[:, 2 * width :]).astype(jnp.bfloat16)

    high, low = split_pair(basis)
    moments = mm(jnp.asarray(high.T), gated) + mm(jnp.asarray(low.T), gated)
    moved = lax.all_to_all(moments, "ctx", split_axis=1, concat_axis=0, tiled=True)
    moved = moved.reshape(peers, NODES, own)

    start = lax.axis_index("ctx") * own
    rates = lax.dynamic_slice_in_dim(decays, start, own, 0)
    weights = lax.dynamic_slice_in_dim(residues, start, own, 0)
    weights = weights * jnp.sqrt(-jnp.expm1(-2.0 * rates))
    into = jnp.exp(-rates[:, :, None] * (rows - 1 - node))
    states = jnp.einsum("djc,crj->dcr", moved, into, precision=lax.Precision.HIGHEST)
    step = jnp.exp(-rates * rows)

    def advance(state, fresh):
        return step * state + fresh, state

    _, held = lax.scan(advance, jnp.zeros_like(states[0]), states)
    out_of = weights[:, :, None] * jnp.exp(-rates[:, :, None] * (1.0 + node))
    past = jnp.einsum("dcr,crj->djc", held, out_of, precision=lax.Precision.HIGHEST)
    past = past.reshape(peers * NODES, own)
    past = lax.all_to_all(past, "ctx", split_axis=0, concat_axis=1, tiled=True)

    all_weights = residues * jnp.sqrt(-jnp.expm1(-2.0 * decays))
    coef = jnp.sum(all_weights[None] * jnp.exp(-decays[None] * node[:, None, None]), 2)
    result = jnp.dot(jnp.asarray(basis, jnp.float32), past, precision=lax.Precision.HIGHEST)
    for j in range(NODES):
        part = mm(jnp.asarray(toeplitz[j].astype(ml_dtypes.bfloat16)), gated)
        result = result + coef[j][None, :] * part
    return queries * result.astype(jnp.bfloat16).astype(jnp.float32)


def solution(mesh):
    in_specs = (P(("dp", "ctx"), None), P(), P(), P())
    out_specs = P(("dp", "ctx"), None)
    return jax.shard_map(shards, mesh=mesh, in_specs=in_specs, out_specs=out_specs, check_vma=False)
```

```python
import functools

import jax
import jax.numpy as jnp
import ml_dtypes
import numpy as np
from jax import lax
from jax.experimental import pallas as pl
from jax.experimental.pallas import tpu as pltpu
from jax.sharding import PartitionSpec as P

F32, BF16 = jnp.float32, jnp.bfloat16
MESH = pl.DeviceIdType.MESH
NODES = 7
CHUNK = 128
GROUP = 16
TOP_RATE = 0.033
LOW_RATE = 3.0517578e-05


def chunk_basis(length):
    rates = 0.5 * TOP_RATE * (1.0 + np.cos(np.linspace(0.0, np.pi, 600)))
    rates = np.clip(rates, LOW_RATE, TOP_RATE)
    family = np.exp(-rates[:, None] * np.arange(length))
    space = np.linalg.svd(family, full_matrices=False)[2][:NODES].T
    rest, picked = space.T.copy(), []
    for _ in range(NODES):
        best = int(np.argmax((rest**2).sum(0)))
        picked.append(best)
        unit = rest[:, best] / np.linalg.norm(rest[:, best])
        rest = rest - np.outer(unit, unit @ rest)
    picked = sorted(picked)
    return picked, space @ np.linalg.inv(space[picked])


def split_pair(table):
    high = table.astype(ml_dtypes.bfloat16)
    low = (table - high.astype(np.float64)).astype(ml_dtypes.bfloat16)
    return high, low


def tables():
    nodes, basis = chunk_basis(CHUNK)
    lag = np.arange(CHUNK)[:, None] - np.arange(CHUNK)[None, :]
    local = np.where(lag[None] >= 0, basis.T[:, np.maximum(lag, 0)], 0.0)
    local = np.concatenate(list(local), 1).astype(ml_dtypes.bfloat16)
    block = np.zeros((2 * CHUNK, 16))
    for half in range(2):
        block[half * CHUNK : (half + 1) * CHUNK, 8 * half : 8 * half + NODES] = basis
    high, low = split_pair(block)
    spread = np.concatenate([high, low], 1)
    gather = np.concatenate([high.T, low.T], 0)
    return nodes, local, gather, spread


def mm(a, b):
    return jnp.dot(a, b, preferred_element_type=F32)


def lanes(start, size):
    return pl.ds(pl.multiple_of(start, 128), size)


def kernel(
    nodes, width, proj_hbm, taps, rates, weights, local, gather, spread, out_hbm,
    proj, halo, shifted, gated, queries, conv, coef, send_m, recv_m, send_t, recv_t, send_g, recv_g,
    into, outof, decay, decay_scan, plain_m, scans, carries, plain_g,
    in_sem, out_sem, halo_send, halo_recv, m_send, m_recv, t_send, t_recv, g_send, g_recv,
):
    ctx = lax.axis_index("ctx")
    peers = lax.axis_size("ctx")
    outer = peers // GROUP
    own = lax.rem(ctx, GROUP)
    row = lax.div(ctx, GROUP)
    base = row * GROUP
    after, before = lax.rem(ctx + 1, peers), lax.rem(ctx + peers - 1, peers)
    part = width // GROUP

    barrier = pltpu.get_barrier_semaphore()

    def greet(device):
        pl.semaphore_signal(barrier, inc=1, device_id={"ctx": device}, device_id_type=MESH)

    greet(after)
    greet(before)

    def greet_group(i, c):
        @pl.when(i != own)
        def _():
            greet(base + i)

        return c

    lax.fori_loop(0, GROUP, greet_group, 0)

    def greet_outer(i, c):
        @pl.when(i != row)
        def _():
            greet(i * GROUP + own)

        return c

    lax.fori_loop(0, outer, greet_outer, 0)

    wide = 512
    steps = width // wide

    def fetch(which, t):
        cols = lanes(which * width + t * wide, wide)
        return pltpu.make_async_copy(proj_hbm.at[:, cols], proj.at[:, cols], in_sem.at[which, t])

    def fetch_all(t, c):
        fetch(1, t).start()
        fetch(2, t).start()
        return c

    lax.fori_loop(0, steps, fetch_all, 0)

    def fetch_q(t, c):
        fetch(0, t).start()
        return c

    lax.fori_loop(0, steps, fetch_q, 0)

    pl.semaphore_wait(barrier, 2 + (GROUP - 1) + (outer - 1))

    rows = proj.shape[0]

    def halo_copy(n, start, size):
        return pltpu.make_async_remote_copy(
            src_ref=proj_hbm.at[pl.ds(rows - 8, 8), pl.ds(start, size)],
            dst_ref=halo.at[:, pl.ds(start, size)],
            send_sem=halo_send.at[n],
            recv_sem=halo_recv.at[n],
            device_id={"ctx": after},
            device_id_type=MESH,
        )

    halo_kv = halo_copy(0, width, 2 * width)
    halo_q = halo_copy(1, 0, width)
    halo_kv.start()
    halo_q.start()

    def amplitude(rate, weight):
        x = 2.0 * rate
        series = 1.0 - x * (0.5 - x * (1 / 6 - x * (1 / 24 - x * (1 / 120 - x * (1 / 720)))))
        return weight * jnp.sqrt(x * series)

    def prepare(t, c):
        cols = lanes(t * wide, wide)
        rate = rates[:, cols]
        amp = amplitude(rate, weights[:, cols])
        for j, n in enumerate(nodes):
            coef[j : j + 1, cols] = jnp.sum(amp * jnp.exp(rate * (-float(n))), axis=0, keepdims=True)
        return c

    lax.fori_loop(0, steps, prepare, 0)

    mine = lanes(own * part, part)
    rate = rates[:, mine]
    amp = amplitude(rate, weights[:, mine])
    for j, n in enumerate(nodes):
        into[16 * j : 16 * j + 16, :] = jnp.exp(rate * (-float(CHUNK - 1 - n)))
        outof[16 * j : 16 * j + 16, :] = amp * jnp.exp(rate * (-float(1 + n)))
    sub = lax.broadcasted_iota(jnp.int32, (8, part), 0)
    far = (sub + 1).astype(F32) * (-float(CHUNK))
    for r in range(16):
        one = jnp.broadcast_to(rate[r : r + 1], (8, part))
        decay[r] = jnp.exp(one * far)
        for k, hop in enumerate((1, 2, 4)):
            decay_scan[3 * r + k] = jnp.where(sub >= hop, jnp.exp(one * (-float(CHUNK * hop))), 0.0)

    halo_kv.wait()
    first = jnp.where(ctx == 0, 0.0, 1.0)

    def lay(slot, start):
        cols = lanes(start, 128)
        shifted[slot, 0:8, :] = halo[:, cols].astype(F32) * first
        for k in range(rows // 16):
            shifted[slot, 8 + 16 * k : 24 + 16 * k, :] = proj[16 * k : 16 * k + 16, cols].astype(F32)

    def tap_rows(start):
        cols = lanes(start, 128)
        block = taps[:, cols]
        return [jnp.broadcast_to(block[j : j + 1], (8, 128)) for j in range(taps.shape[0])]

    def filtered(slot, k, weights_j):
        total = None
        for j, w in enumerate(weights_j):
            term = shifted[slot, 8 + 8 * k - j : 16 + 8 * k - j, :] * w
            total = term if total is None else total + term
        return total

    def moment_copy(o):
        return pltpu.make_async_remote_copy(
            src_ref=send_m.at[o],
            dst_ref=recv_m.at[own],
            send_sem=m_send.at[o],
            recv_sem=m_recv.at[own],
            device_id={"ctx": base + o},
            device_id_type=MESH,
        )

    def moments(o):
        both = mm(gather[...], gated[:, lanes(o * part, part)])
        return (both[:16] + both[16:]).astype(BF16)

    def send_moments(o, value):
        send_m[o] = value

        @pl.when(o == own)
        def _():
            recv_m[own] = value

        @pl.when(o != own)
        def _():
            moment_copy(o).start()

    def gate(i, c):
        @pl.when(lax.rem(i, wide // part) == 0)
        def _():
            t = lax.div(i, wide // part)
            fetch(1, t).wait()
            fetch(2, t).wait()

        last = jnp.maximum(i - 1, 0)
        ready = moments(last)
        for h in range(part // 128):
            at = i * part + 128 * h
            lay(2 * h, width + at)
            lay(2 * h + 1, 2 * width + at)
            tk, tv = tap_rows(width + at), tap_rows(2 * width + at)
            for k in range(rows // 16):
                pair = [filtered(2 * h, 2 * k + b, tk) * filtered(2 * h + 1, 2 * k + b, tv) for b in range(2)]
                gated[16 * k : 16 * k + 16, lanes(at, 128)] = jnp.concatenate(pair, 0).astype(BF16)

        @pl.when(i > 0)
        def _():
            send_moments(last, ready)

        return c

    lax.fori_loop(0, GROUP, gate, 0)
    send_moments(GROUP - 1, moments(GROUP - 1))
    halo_q.wait()

    def total_copy(x):
        return pltpu.make_async_remote_copy(
            src_ref=send_t,
            dst_ref=recv_t.at[row],
            send_sem=t_send.at[x],
            recv_sem=t_recv.at[row],
            device_id={"ctx": x * GROUP + own},
            device_id_type=MESH,
        )

    def total_arrival(x):
        return pltpu.make_async_remote_copy(
            src_ref=send_t,
            dst_ref=recv_t.at[x],
            send_sem=t_send.at[x],
            recv_sem=t_recv.at[x],
            device_id={"ctx": x * GROUP + own},
            device_id_type=MESH,
        )

    def moment_arrival(s):
        return pltpu.make_async_remote_copy(
            src_ref=send_m.at[s],
            dst_ref=recv_m.at[s],
            send_sem=m_send.at[s],
            recv_sem=m_recv.at[s],
            device_id={"ctx": base + s},
            device_id_type=MESH,
        )

    def past_copy(d):
        return pltpu.make_async_remote_copy(
            src_ref=send_g.at[d],
            dst_ref=recv_g.at[own],
            send_sem=g_send.at[d],
            recv_sem=g_recv.at[own],
            device_id={"ctx": base + d},
            device_id_type=MESH,
        )

    def past_arrival(s):
        return pltpu.make_async_remote_copy(
            src_ref=send_g.at[s],
            dst_ref=recv_g.at[s],
            send_sem=g_send.at[s],
            recv_sem=g_recv.at[s],
            device_id={"ctx": base + s},
            device_id_type=MESH,
        )

    halves = part // 128
    sub128 = lax.broadcasted_iota(jnp.int32, (8, 128), 0)

    def gather_states():
        def arrive(s, c):
            @pl.when(s != own)
            def _():
                moment_arrival(s).wait()

            return c

        lax.fori_loop(0, GROUP, arrive, 0)
        for s in range(GROUP):
            block = recv_m[s].astype(F32)
            for h in range(halves):
                plain_m[h, 16 * s : 16 * s + 16, :] = block[:, 128 * h : 128 * h + 128]

        for h in range(halves):
            cols = slice(128 * h, 128 * h + 128)

            def scan_group(g, c, h=h, cols=cols):
                m = [plain_m[h, pl.ds(g * 64 + j, 8, stride=8), :] for j in range(NODES)]
                for r in range(16):
                    state = None
                    for j in range(NODES):
                        term = m[j] * into[16 * j + r : 16 * j + r + 1, cols]
                        state = term if state is None else state + term
                    for k, hop in enumerate((1, 2, 4)):
                        state = state + decay_scan[3 * r + k, :, cols] * pltpu.roll(state, hop, 0)
                    scans[h, pl.ds(pl.multiple_of(r * 32 + 8 * g, 8), 8), :] = state
                return c

            lax.fori_loop(0, 4, scan_group, 0)
            step8 = jnp.exp(rates[:, lanes(own * part + 128 * h, 128)] * (-float(8 * CHUNK)))
            total = scans[h, pl.ds(7, 16, stride=32), :]
            for g in range(1, 4):
                total = total * step8 + scans[h, pl.ds(8 * g + 7, 16, stride=32), :]
            send_t[:, cols] = total

        def send(x, c):
            @pl.when(x != row)
            def _():
                total_copy(x).start()

            return c

        lax.fori_loop(0, outer, send, 0)

    def spread_states():
        def arrive(x, c):
            @pl.when(x != row)
            def _():
                total_arrival(x).wait()

            return c

        lax.fori_loop(0, outer, arrive, 0)
        for h in range(halves):
            cols = slice(128 * h, 128 * h + 128)
            rate = rates[:, lanes(own * part + 128 * h, 128)]
            step8 = jnp.exp(rate * (-float(8 * CHUNK)))
            step32 = jnp.exp(rate * (-float(32 * CHUNK)))
            held = jnp.zeros((16, 128), F32)
            for x in range(outer - 1):
                held = jnp.where(x < row, held * step32 + recv_t[x, :, cols], held)
            for g in range(4):
                carries[h, 16 * g : 16 * g + 16, :] = held
                held = held * step8 + scans[h, pl.ds(8 * g + 7, 16, stride=32), :]

            def spread_group(g, c, h=h, cols=cols):
                states = []
                for r in range(16):
                    carry = jnp.broadcast_to(carries[h, pl.ds(16 * g + r, 1), :], (8, 128))
                    full = scans[h, pl.ds(pl.multiple_of(r * 32 + 8 * g, 8), 8), :] + decay[r, :, cols] * carry
                    states.append(jnp.where(sub128 == 0, carry, pltpu.roll(full, 1, 0)))
                for j in range(NODES):
                    past = None
                    for r in range(16):
                        term = states[r] * outof[16 * j + r : 16 * j + r + 1, cols]
                        past = term if past is None else past + term
                    plain_g[h, pl.ds(g * 64 + j, 8, stride=8), :] = past
                plain_g[h, pl.ds(g * 64 + NODES, 8, stride=8), :] = jnp.zeros((8, 128), F32)
                return c

            lax.fori_loop(0, 4, spread_group, 0)
        for d in range(GROUP):
            for h in range(halves):
                send_g[d, :, 128 * h : 128 * h + 128] = plain_g[h, 16 * d : 16 * d + 16, :].astype(BF16)
        recv_g[own] = send_g[own]

        def send(d, c):
            @pl.when(d != own)
            def _():
                past_copy(d).start()

            return c

        lax.fori_loop(0, GROUP, send, 0)

    def within(t, c):
        fetch(0, t).wait()

        @pl.when(t == 2)
        def _():
            gather_states()

        @pl.when(t == 5)
        def _():
            spread_states()

        for piece in range(2):
            cols = lanes(t * wide + 256 * piece, 256)
            scale = coef[:, cols].astype(BF16)
            for half in range(2):
                tokens = slice(half * CHUNK, (half + 1) * CHUNK)
                field = gated[tokens, cols]
                stacked = jnp.concatenate([field * scale[j : j + 1] for j in range(NODES)], 0)
                result = mm(local[...], stacked)
                at = t * wide + 256 * piece + 128 * half
                slot = 2 * piece + half
                lay(slot, at)
                tq = tap_rows(at)
                for k in range(rows // 8):
                    queries[8 * k : 8 * k + 8, lanes(at, 128)] = filtered(slot, k, tq)
                conv[tokens, cols] = result
        return c

    lax.fori_loop(0, steps, within, 0)

    def store(t):
        cols = lanes(t * wide, wide)
        return pltpu.make_async_copy(queries.at[:, cols], out_hbm.at[:, cols], out_sem.at[t])

    def finish(t, c):
        per = wide // part
        for b in range(per):
            o = per * t + b

            @pl.when(o != own)
            def _(o=o):
                past_arrival(o).wait()

        for b in range(per):
            o = per * t + b
            cols = lanes(o * part, part)
            past = recv_g[o]
            result = mm(spread[...], jnp.concatenate([past, past], 0))
            queries[:, cols] = queries[:, cols] * (conv[:, cols] + result)
        store(t).start()
        return c

    lax.fori_loop(0, steps, finish, 0)

    def close_out(t, c):
        store(t).wait()
        return c

    lax.fori_loop(0, steps, close_out, 0)


def shards(projected, taps, decays, residues):
    rows = projected.shape[0]
    width = taps.shape[1] // 3
    part = width // GROUP
    outer = lax.axis_size("ctx") // GROUP
    nodes, local, gather, spread = tables()
    turned = jnp.concatenate([decays, residues], 1).T
    rates, weights = turned[:16], turned[16:]
    vmem = pl.BlockSpec(memory_space=pltpu.VMEM)
    hbm = pl.BlockSpec(memory_space=pl.ANY)
    dma = pltpu.SemaphoreType.DMA
    steps = width // 512
    return pl.pallas_call(
        functools.partial(kernel, nodes, width),
        out_shape=jax.ShapeDtypeStruct((rows, width), F32),
        in_specs=[hbm, vmem, vmem, vmem, vmem, vmem, vmem],
        out_specs=hbm,
        scratch_shapes=[
            pltpu.VMEM((rows, 3 * width), BF16),
            pltpu.VMEM((8, 3 * width), BF16),
            pltpu.VMEM((4, rows + 8, 128), F32),
            pltpu.VMEM((rows, width), BF16),
            pltpu.VMEM((rows, width), F32),
            pltpu.VMEM((rows, width), F32),
            pltpu.VMEM((8, width), F32),
            pltpu.VMEM((GROUP, 16, part), BF16),
            pltpu.VMEM((GROUP, 16, part), BF16),
            pltpu.VMEM((16, part), F32),
            pltpu.VMEM((outer, 16, part), F32),
            pltpu.VMEM((GROUP, 16, part), BF16),
            pltpu.VMEM((GROUP, 16, part), BF16),
            pltpu.VMEM((16 * NODES, part), F32),
            pltpu.VMEM((16 * NODES, part), F32),
            pltpu.VMEM((16, 8, part), F32),
            pltpu.VMEM((48, 8, part), F32),
            pltpu.VMEM((part // 128, 256, 128), F32),
            pltpu.VMEM((part // 128, 512, 128), F32),
            pltpu.VMEM((part // 128, 64, 128), F32),
            pltpu.VMEM((part // 128, 256, 128), F32),
            dma((3, steps)), dma((steps,)),
            dma((2,)), dma((2,)),
            dma((GROUP,)), dma((GROUP,)),
            dma((outer,)), dma((outer,)),
            dma((GROUP,)), dma((GROUP,)),
        ],
        compiler_params=pltpu.CompilerParams(
            collective_id=0, has_side_effects=True, vmem_limit_bytes=48 * 2**20
        ),
        name="hyena",
    )(projected, taps, rates, weights, jnp.asarray(local), jnp.asarray(gather), jnp.asarray(spread))


def solution(mesh):
    in_specs = (P(("dp", "ctx"), None), P(), P(), P())
    out_specs = P(("dp", "ctx"), None)
    return jax.shard_map(shards, mesh=mesh, in_specs=in_specs, out_specs=out_specs, check_vma=False)
```

```python
import functools

import jax
import jax.numpy as jnp
import ml_dtypes
import numpy as np
from jax import lax
from jax.experimental import pallas as pl
from jax.experimental.pallas import tpu as pltpu
from jax.sharding import PartitionSpec as P

F32, BF16 = jnp.float32, jnp.bfloat16
MESH = pl.DeviceIdType.MESH
NODES = 7
CHUNK = 128
GROUP = 16
TOP_RATE = 0.033
LOW_RATE = 3.0517578e-05


def chunk_basis(length):
    rates = 0.5 * TOP_RATE * (1.0 + np.cos(np.linspace(0.0, np.pi, 600)))
    rates = np.clip(rates, LOW_RATE, TOP_RATE)
    family = np.exp(-rates[:, None] * np.arange(length))
    space = np.linalg.svd(family, full_matrices=False)[2][:NODES].T
    rest, picked = space.T.copy(), []
    for _ in range(NODES):
        best = int(np.argmax((rest**2).sum(0)))
        picked.append(best)
        unit = rest[:, best] / np.linalg.norm(rest[:, best])
        rest = rest - np.outer(unit, unit @ rest)
    picked = sorted(picked)
    return picked, space @ np.linalg.inv(space[picked])


def split_pair(table):
    high = table.astype(ml_dtypes.bfloat16)
    low = (table - high.astype(np.float64)).astype(ml_dtypes.bfloat16)
    return high, low


def tables():
    nodes, basis = chunk_basis(CHUNK)
    lag = np.arange(CHUNK)[:, None] - np.arange(CHUNK)[None, :]
    local = np.where(lag[None] >= 0, basis.T[:, np.maximum(lag, 0)], 0.0)
    local = np.concatenate(list(local), 1).astype(ml_dtypes.bfloat16)
    block = np.zeros((2 * CHUNK, 16))
    for half in range(2):
        block[half * CHUNK : (half + 1) * CHUNK, 8 * half : 8 * half + NODES] = basis
    high, low = split_pair(block)
    spread = np.concatenate([high, low], 1)
    gather = np.concatenate([high.T, low.T], 0)
    return nodes, local, gather, spread


def mm(a, b):
    return jnp.dot(a, b, preferred_element_type=F32)


def lanes(start, size):
    return pl.ds(pl.multiple_of(start, 128), size)


def kernel(
    nodes, width, proj_hbm, taps_hbm, rates_hbm, weights_hbm, local_hbm, gather_hbm, spread_hbm, queries,
    taps, rates, weights, local, gather, spread,
    proj, halo, shifted, gated, conv, coef, send_m, recv_m, send_t, recv_t, send_g, recv_g,
    into, outof, decay, decay_scan, plain_m, scans, carries, plain_g,
    small_sem, in_sem, halo_send, halo_recv, m_send, m_recv, t_send, t_recv, g_send, g_recv,
):
    ctx = lax.axis_index("ctx")
    peers = lax.axis_size("ctx")
    outer = peers // GROUP
    own = lax.rem(ctx, GROUP)
    row = lax.div(ctx, GROUP)
    base = row * GROUP
    after, before = lax.rem(ctx + 1, peers), lax.rem(ctx + peers - 1, peers)
    part = width // GROUP

    barrier = pltpu.get_barrier_semaphore()

    def greet(device):
        pl.semaphore_signal(barrier, inc=1, device_id={"ctx": device}, device_id_type=MESH)

    greet(after)
    greet(before)

    def greet_group(i, c):
        @pl.when(i != own)
        def _():
            greet(base + i)

        return c

    lax.fori_loop(0, GROUP, greet_group, 0)

    def greet_outer(i, c):
        @pl.when(i != row)
        def _():
            greet(i * GROUP + own)

        return c

    lax.fori_loop(0, outer, greet_outer, 0)

    pairs = (
        (rates_hbm, rates), (weights_hbm, weights), (taps_hbm, taps),
        (gather_hbm, gather), (local_hbm, local), (spread_hbm, spread),
    )
    small = [pltpu.make_async_copy(a, b, small_sem.at[n]) for n, (a, b) in enumerate(pairs)]
    small[2].start()

    wide = 512
    steps = width // wide

    def fetch(which, t):
        cols = lanes(which * width + t * wide, wide)
        return pltpu.make_async_copy(proj_hbm.at[:, cols], proj.at[:, cols], in_sem.at[which, t])

    def fetch_all(t, c):
        fetch(1, t).start()
        fetch(2, t).start()
        return c

    lax.fori_loop(0, steps, fetch_all, 0)

    def fetch_q(t, c):
        fetch(0, t).start()
        return c

    for n in (3, 0, 1, 4, 5):
        small[n].start()
    lax.fori_loop(0, steps, fetch_q, 0)

    rows = proj.shape[0]

    def halo_copy(n, start, size):
        return pltpu.make_async_remote_copy(
            src_ref=proj_hbm.at[pl.ds(rows - 8, 8), pl.ds(start, size)],
            dst_ref=halo.at[:, pl.ds(start, size)],
            send_sem=halo_send.at[n],
            recv_sem=halo_recv.at[n],
            device_id={"ctx": after},
            device_id_type=MESH,
        )

    quarter = width // 4
    halo_q = halo_copy(8, 0, width)
    halo_kv = [halo_copy(n, (1 + n % 2) * width + (n // 2) * quarter, quarter) for n in range(8)]
    pl.semaphore_wait(barrier, 2 + (GROUP - 1) + (outer - 1))
    for piece in halo_kv:
        piece.start()
    halo_q.start()

    def amplitude(rate, weight):
        x = 2.0 * rate
        series = 1.0 - x * (0.5 - x * (1 / 6 - x * (1 / 24 - x * (1 / 120 - x * (1 / 720)))))
        return weight * jnp.sqrt(x * series)

    def prepare(t):
        cols = lanes(t * wide, wide)
        rate = rates[:, cols]
        amp = amplitude(rate, weights[:, cols])
        for j, n in enumerate(nodes):
            coef[j : j + 1, cols] = jnp.sum(amp * jnp.exp(rate * (-float(n))), axis=0, keepdims=True)


    def owner_tables():
        mine = lanes(own * part, part)
        rate = rates[:, mine]
        amp = amplitude(rate, weights[:, mine])
        for j, n in enumerate(nodes):
            into[16 * j : 16 * j + 16, :] = jnp.exp(rate * (-float(CHUNK - 1 - n)))
            outof[16 * j : 16 * j + 16, :] = amp * jnp.exp(rate * (-float(1 + n)))
        sub = lax.broadcasted_iota(jnp.int32, (8, part), 0)
        far = (sub + 1).astype(F32) * (-float(CHUNK))
        for r in range(16):
            one = jnp.broadcast_to(rate[r : r + 1], (8, part))
            decay[r] = jnp.exp(one * far)
            for k, hop in enumerate((1, 2, 4)):
                decay_scan[3 * r + k] = jnp.where(sub >= hop, jnp.exp(one * (-float(CHUNK * hop))), 0.0)

    small[2].wait()
    small[3].wait()

    def lay(slot, start, edge):
        cols = lanes(start, 128)
        if edge:
            shifted[slot, 0:8, :] = jnp.where(ctx == 0, 0.0, halo[:, cols].astype(F32))
        for k in range(1 if edge == "only" else rows // 16):
            shifted[slot, 8 + 16 * k : 24 + 16 * k, :] = proj[16 * k : 16 * k + 16, cols].astype(F32)

    def tap_rows(start):
        cols = lanes(start, 128)
        block = taps[:, cols]
        return [jnp.broadcast_to(block[j : j + 1], (8, 128)) for j in range(taps.shape[0])]

    def filtered(slot, k, weights_j):
        total = None
        for j, w in enumerate(weights_j):
            term = shifted[slot, 8 + 8 * k - j : 16 + 8 * k - j, :] * w
            total = term if total is None else total + term
        return total

    def moment_copy(o):
        return pltpu.make_async_remote_copy(
            src_ref=send_m.at[o],
            dst_ref=recv_m.at[own],
            send_sem=m_send.at[o],
            recv_sem=m_recv.at[own],
            device_id={"ctx": base + o},
            device_id_type=MESH,
        )

    def moments(o):
        both = mm(gather[...], gated[:, lanes(o * part, part)])
        return (both[:16] + both[16:]).astype(BF16)

    def send_moments(o, value):
        send_m[o] = value

        @pl.when(o == own)
        def _():
            recv_m[own] = value

        @pl.when(o != own)
        def _():
            moment_copy(o).start()

    blocks = part // 128

    def edge_gate(o):
        for h in range(blocks):
            at = o * part + 128 * h
            lay(2 * blocks + 2 * h, width + at, "only")
            lay(2 * blocks + 2 * h + 1, 2 * width + at, "only")
            tk, tv = tap_rows(width + at), tap_rows(2 * width + at)
            both = filtered(2 * blocks + 2 * h, 0, tk) * filtered(2 * blocks + 2 * h + 1, 0, tv)
            gated[0:8, lanes(at, 128)] = both.astype(BF16)

    lag = 6
    per_quarter = quarter // part

    def gate(i, c):
        @pl.when(lax.rem(i, wide // part) == 0)
        def _():
            t = lax.div(i, wide // part)
            fetch(1, t).wait()
            fetch(2, t).wait()

        @pl.when(i == 3)
        def _():
            small[0].wait()
            small[1].wait()
            owner_tables()

        for n in range(4):
            if lag + n * per_quarter < GROUP:

                @pl.when(i == lag + n * per_quarter)
                def _(n=n):
                    halo_kv[2 * n].wait()
                    halo_kv[2 * n + 1].wait()

        @pl.when(i >= lag)
        def _():
            edge_gate(i - lag)
            send_moments(i - lag, moments(i - lag))

        for h in range(blocks):
            at = i * part + 128 * h
            lay(2 * h, width + at, None)
            lay(2 * h + 1, 2 * width + at, None)
            tk, tv = tap_rows(width + at), tap_rows(2 * width + at)
            for k in range(rows // 16):
                pair = [
                    filtered(2 * h, 2 * k + b, tk) * filtered(2 * h + 1, 2 * k + b, tv)
                    if k + b > 0
                    else jnp.zeros((8, 128), F32)
                    for b in range(2)
                ]
                gated[16 * k : 16 * k + 16, lanes(at, 128)] = jnp.concatenate(pair, 0).astype(BF16)
        return c

    lax.fori_loop(0, GROUP, gate, 0)

    for n in range(4):
        if lag + n * per_quarter >= GROUP:
            halo_kv[2 * n].wait()
            halo_kv[2 * n + 1].wait()
    for o in range(GROUP - lag, GROUP):
        edge_gate(o)
    for o in range(GROUP - lag, GROUP):
        send_moments(o, moments(o))
    small[4].wait()
    small[5].wait()
    halo_q.wait()

    def total_copy(x):
        return pltpu.make_async_remote_copy(
            src_ref=send_t,
            dst_ref=recv_t.at[row],
            send_sem=t_send.at[x],
            recv_sem=t_recv.at[row],
            device_id={"ctx": x * GROUP + own},
            device_id_type=MESH,
        )

    def total_arrival(x):
        return pltpu.make_async_remote_copy(
            src_ref=send_t,
            dst_ref=recv_t.at[x],
            send_sem=t_send.at[x],
            recv_sem=t_recv.at[x],
            device_id={"ctx": x * GROUP + own},
            device_id_type=MESH,
        )

    def moment_arrival(s):
        return pltpu.make_async_remote_copy(
            src_ref=send_m.at[s],
            dst_ref=recv_m.at[s],
            send_sem=m_send.at[s],
            recv_sem=m_recv.at[s],
            device_id={"ctx": base + s},
            device_id_type=MESH,
        )

    def past_copy(d):
        return pltpu.make_async_remote_copy(
            src_ref=send_g.at[d],
            dst_ref=recv_g.at[own],
            send_sem=g_send.at[d],
            recv_sem=g_recv.at[own],
            device_id={"ctx": base + d},
            device_id_type=MESH,
        )

    def past_arrival(s):
        return pltpu.make_async_remote_copy(
            src_ref=send_g.at[s],
            dst_ref=recv_g.at[s],
            send_sem=g_send.at[s],
            recv_sem=g_recv.at[s],
            device_id={"ctx": base + s},
            device_id_type=MESH,
        )

    halves = part // 128
    sub128 = lax.broadcasted_iota(jnp.int32, (8, 128), 0)

    def gather_states():
        def arrive(s, c):
            @pl.when(s != own)
            def _():
                moment_arrival(s).wait()

            return c

        lax.fori_loop(0, GROUP, arrive, 0)
        for s in range(GROUP):
            block = recv_m[s].astype(F32)
            for h in range(halves):
                plain_m[h, 16 * s : 16 * s + 16, :] = block[:, 128 * h : 128 * h + 128]

        for h in range(halves):
            cols = slice(128 * h, 128 * h + 128)

            def scan_group(g, c, h=h, cols=cols):
                m = [plain_m[h, pl.ds(g * 64 + j, 8, stride=8), :] for j in range(NODES)]
                for r in range(16):
                    state = None
                    for j in range(NODES):
                        term = m[j] * into[16 * j + r : 16 * j + r + 1, cols]
                        state = term if state is None else state + term
                    for k, hop in enumerate((1, 2, 4)):
                        state = state + decay_scan[3 * r + k, :, cols] * pltpu.roll(state, hop, 0)
                    scans[h, pl.ds(pl.multiple_of(r * 32 + 8 * g, 8), 8), :] = state
                return c

            lax.fori_loop(0, 4, scan_group, 0)
            step8 = jnp.exp(rates[:, lanes(own * part + 128 * h, 128)] * (-float(8 * CHUNK)))
            total = scans[h, pl.ds(7, 16, stride=32), :]
            for g in range(1, 4):
                total = total * step8 + scans[h, pl.ds(8 * g + 7, 16, stride=32), :]
            send_t[:, cols] = total

        def send(x, c):
            @pl.when(x != row)
            def _():
                total_copy(x).start()

            return c

        lax.fori_loop(0, outer, send, 0)

    def spread_states():
        def arrive(x, c):
            @pl.when(x != row)
            def _():
                total_arrival(x).wait()

            return c

        lax.fori_loop(0, outer, arrive, 0)
        for h in range(halves):
            cols = slice(128 * h, 128 * h + 128)
            rate = rates[:, lanes(own * part + 128 * h, 128)]
            step8 = jnp.exp(rate * (-float(8 * CHUNK)))
            step32 = jnp.exp(rate * (-float(32 * CHUNK)))
            held = jnp.zeros((16, 128), F32)
            for x in range(outer - 1):
                held = jnp.where(x < row, held * step32 + recv_t[x, :, cols], held)
            for g in range(4):
                carries[h, 16 * g : 16 * g + 16, :] = held
                held = held * step8 + scans[h, pl.ds(8 * g + 7, 16, stride=32), :]

        def spread_group(n, c):
            g = lax.rem(n + lax.div(own, 4), 4)
            for h in range(halves):
                cols = slice(128 * h, 128 * h + 128)
                states = []
                for r in range(16):
                    carry = jnp.broadcast_to(carries[h, pl.ds(16 * g + r, 1), :], (8, 128))
                    full = scans[h, pl.ds(pl.multiple_of(r * 32 + 8 * g, 8), 8), :] + decay[r, :, cols] * carry
                    states.append(jnp.where(sub128 == 0, carry, pltpu.roll(full, 1, 0)))
                for j in range(NODES):
                    past = None
                    for r in range(16):
                        term = states[r] * outof[16 * j + r : 16 * j + r + 1, cols]
                        past = term if past is None else past + term
                    plain_g[h, pl.ds(g * 64 + j, 8, stride=8), :] = past
                plain_g[h, pl.ds(g * 64 + NODES, 8, stride=8), :] = jnp.zeros((8, 128), F32)
            for b in range(4):
                d = 4 * g + b
                for h in range(halves):
                    block = plain_g[h, pl.ds(pl.multiple_of(16 * d, 16), 16), :]
                    send_g[d, :, 128 * h : 128 * h + 128] = block.astype(BF16)

            def send(b, c):
                d = 4 * g + lax.rem(b + own, 4)

                @pl.when(d == own)
                def _():
                    recv_g[own] = send_g[d]

                @pl.when(d != own)
                def _():
                    past_copy(d).start()

                return c

            lax.fori_loop(0, 4, send, 0)
            return c

        lax.fori_loop(0, 4, spread_group, 0)

    def within(t, c):
        fetch(0, t).wait()

        @pl.when(t == 0)
        def _():
            gather_states()

        @pl.when(t == 3)
        def _():
            spread_states()

        prepare(t)
        for piece in range(2):
            cols = lanes(t * wide + 256 * piece, 256)
            scale = coef[:, cols].astype(BF16)
            for half in range(2):
                tokens = slice(half * CHUNK, (half + 1) * CHUNK)
                field = gated[tokens, cols]
                stacked = jnp.concatenate([field * scale[j : j + 1] for j in range(NODES)], 0)
                result = mm(local[...], stacked)
                at = t * wide + 256 * piece + 128 * half
                slot = 2 * piece + half
                lay(slot, at, "all")
                tq = tap_rows(at)
                for k in range(rows // 8):
                    queries[8 * k : 8 * k + 8, lanes(at, 128)] = filtered(slot, k, tq)
                conv[tokens, cols] = result
        return c

    lax.fori_loop(0, steps, within, 0)

    def finish(t, c):
        per = wide // part
        for b in range(per):
            o = per * t + b

            @pl.when(o != own)
            def _(o=o):
                past_arrival(o).wait()

        for b in range(per):
            o = per * t + b
            cols = lanes(o * part, part)
            past = recv_g[o]
            past = jnp.concatenate([past, past], 0)
            for p in range(rows // CHUNK):
                tokens = slice(p * CHUNK, (p + 1) * CHUNK)
                result = mm(spread[tokens, :], past)
                queries[tokens, cols] = queries[tokens, cols] * (conv[tokens, cols] + result)
        return c

    lax.fori_loop(0, steps, finish, 0)


def shards(projected, taps, decays, residues):
    rows = projected.shape[0]
    width = taps.shape[1] // 3
    part = width // GROUP
    outer = lax.axis_size("ctx") // GROUP
    nodes, local, gather, spread = tables()
    turned = jnp.concatenate([decays, residues], 1).T
    rates, weights = turned[:16], turned[16:]
    hbm = pl.BlockSpec(memory_space=pltpu.HBM)
    dma = pltpu.SemaphoreType.DMA
    steps = width // 512
    return pl.pallas_call(
        functools.partial(kernel, nodes, width),
        out_shape=pltpu.VMEM((rows, width), F32),
        in_specs=[hbm] * 7,
        out_specs=pl.BlockSpec(memory_space=pltpu.VMEM),
        scratch_shapes=[
            pltpu.VMEM(taps.shape, F32),
            pltpu.VMEM(rates.shape, F32),
            pltpu.VMEM(weights.shape, F32),
            pltpu.VMEM(local.shape, BF16),
            pltpu.VMEM(gather.shape, BF16),
            pltpu.VMEM(spread.shape, BF16),
            pltpu.VMEM((rows, 3 * width), BF16),
            pltpu.VMEM((8, 3 * width), BF16),
            pltpu.VMEM((8, rows + 8, 128), F32),
            pltpu.VMEM((rows, width), BF16),
            pltpu.VMEM((rows, width), F32),
            pltpu.VMEM((8, width), F32),
            pltpu.VMEM((GROUP, 16, part), BF16),
            pltpu.VMEM((GROUP, 16, part), BF16),
            pltpu.VMEM((16, part), F32),
            pltpu.VMEM((outer, 16, part), F32),
            pltpu.VMEM((GROUP, 16, part), BF16),
            pltpu.VMEM((GROUP, 16, part), BF16),
            pltpu.VMEM((16 * NODES, part), F32),
            pltpu.VMEM((16 * NODES, part), F32),
            pltpu.VMEM((16, 8, part), F32),
            pltpu.VMEM((48, 8, part), F32),
            pltpu.VMEM((part // 128, 256, 128), F32),
            pltpu.VMEM((part // 128, 512, 128), F32),
            pltpu.VMEM((part // 128, 64, 128), F32),
            pltpu.VMEM((part // 128, 256, 128), F32),
            dma((6,)), dma((3, steps)),
            dma((9,)), dma((9,)),
            dma((GROUP,)), dma((GROUP,)),
            dma((outer,)), dma((outer,)),
            dma((GROUP,)), dma((GROUP,)),
        ],
        compiler_params=pltpu.CompilerParams(
            collective_id=0, has_side_effects=True, vmem_limit_bytes=60800 * 2**10
        ),
        name="hyena",
    )(projected, taps, rates, weights, jnp.asarray(local), jnp.asarray(gather), jnp.asarray(spread))


def solution(mesh):
    in_specs = (P(("dp", "ctx"), None), P(), P(), P())
    out_specs = P(("dp", "ctx"), None)
    return jax.shard_map(shards, mesh=mesh, in_specs=in_specs, out_specs=out_specs, check_vma=False)
```

```python
import functools

import jax
import jax.numpy as jnp
import ml_dtypes
import numpy as np
from jax import lax
from jax.experimental import pallas as pl
from jax.experimental.pallas import tpu as pltpu
from jax.sharding import PartitionSpec as P

F32, BF16 = jnp.float32, jnp.bfloat16
MESH = pl.DeviceIdType.MESH
NODES = 7
CHUNK = 128
GROUP = 16
TOP_RATE = 0.033
LOW_RATE = 3.0517578e-05


def chunk_basis(length):
    rates = 0.5 * TOP_RATE * (1.0 + np.cos(np.linspace(0.0, np.pi, 600)))
    rates = np.clip(rates, LOW_RATE, TOP_RATE)
    family = np.exp(-rates[:, None] * np.arange(length))
    space = np.linalg.svd(family, full_matrices=False)[2][:NODES].T
    rest, picked = space.T.copy(), []
    for _ in range(NODES):
        best = int(np.argmax((rest**2).sum(0)))
        picked.append(best)
        unit = rest[:, best] / np.linalg.norm(rest[:, best])
        rest = rest - np.outer(unit, unit @ rest)
    picked = sorted(picked)
    return picked, space @ np.linalg.inv(space[picked])


def split_pair(table):
    high = table.astype(ml_dtypes.bfloat16)
    low = (table - high.astype(np.float64)).astype(ml_dtypes.bfloat16)
    return high, low


def tables():
    nodes, basis = chunk_basis(CHUNK)
    lag = np.arange(CHUNK)[:, None] - np.arange(CHUNK)[None, :]
    local = np.where(lag[None] >= 0, basis.T[:, np.maximum(lag, 0)], 0.0)
    local = np.concatenate(list(local), 1).astype(ml_dtypes.bfloat16)
    block = np.zeros((2 * CHUNK, 16))
    for half in range(2):
        block[half * CHUNK : (half + 1) * CHUNK, 8 * half : 8 * half + NODES] = basis
    high, low = split_pair(block)
    spread = np.concatenate([high, low], 1)
    gather = np.concatenate([high.T, low.T], 0)
    return nodes, local, gather, spread


def mm(a, b):
    return jnp.dot(a, b, preferred_element_type=F32)


def lanes(start, size):
    return pl.ds(pl.multiple_of(start, 128), size)


def kernel(
    nodes, width, proj_hbm, taps_hbm, modes_hbm, local_hbm, gather_hbm, spread_hbm, queries,
    taps, rates, weights, local, gather, spread,
    proj, halo, shifted, gated, conv, coef, send_m, recv_m, send_t, recv_t, send_g, recv_g,
    into, outof, decay, decay_scan, plain_m, scans, carries, plain_g,
    small_sem, in_sem, halo_send, halo_recv, m_send, m_recv, t_send, t_recv, g_send, g_recv,
):
    ctx = lax.axis_index("ctx")
    peers = lax.axis_size("ctx")
    outer = peers // GROUP
    own = lax.rem(ctx, GROUP)
    row = lax.div(ctx, GROUP)
    base = row * GROUP
    after, before = lax.rem(ctx + 1, peers), lax.rem(ctx + peers - 1, peers)
    part = width // GROUP

    barrier = pltpu.get_barrier_semaphore()

    def greet(device):
        pl.semaphore_signal(barrier, inc=1, device_id={"ctx": device}, device_id_type=MESH)

    greet(after)
    greet(before)

    def greet_group(i, c):
        @pl.when(i != own)
        def _():
            greet(base + i)

        return c

    lax.fori_loop(0, GROUP, greet_group, 0)

    def greet_outer(i, c):
        @pl.when(i != row)
        def _():
            greet(i * GROUP + own)

        return c

    lax.fori_loop(0, outer, greet_outer, 0)

    pairs = (
        (modes_hbm.at[0:16], rates), (modes_hbm.at[16:32], weights), (taps_hbm, taps),
        (gather_hbm, gather), (local_hbm, local), (spread_hbm, spread),
    )
    small = [pltpu.make_async_copy(a, b, small_sem.at[n]) for n, (a, b) in enumerate(pairs)]
    small[2].start()

    wide = 512
    steps = width // wide

    def fetch(which, t):
        cols = lanes(which * width + t * wide, wide)
        return pltpu.make_async_copy(proj_hbm.at[:, cols], proj.at[:, cols], in_sem.at[which, t])

    def fetch_all(t, c):
        fetch(1, t).start()
        fetch(2, t).start()
        return c

    lax.fori_loop(0, steps, fetch_all, 0)

    def fetch_q(t, c):
        fetch(0, t).start()
        return c

    for n in (3, 0, 1, 4, 5):
        small[n].start()
    lax.fori_loop(0, steps, fetch_q, 0)

    rows = proj.shape[0]

    def halo_copy(n, start, size):
        return pltpu.make_async_remote_copy(
            src_ref=proj_hbm.at[pl.ds(rows - 8, 8), pl.ds(start, size)],
            dst_ref=halo.at[:, pl.ds(start, size)],
            send_sem=halo_send.at[n],
            recv_sem=halo_recv.at[n],
            device_id={"ctx": after},
            device_id_type=MESH,
        )

    quarter = width // 4
    halo_q = halo_copy(8, 0, width)
    halo_kv = [halo_copy(n, (1 + n % 2) * width + (n // 2) * quarter, quarter) for n in range(8)]
    pl.semaphore_wait(barrier, 2 + (GROUP - 1) + (outer - 1))
    for piece in halo_kv:
        piece.start()
    halo_q.start()

    def amplitude(rate, weight):
        x = 2.0 * rate
        series = 1.0 - x * (0.5 - x * (1 / 6 - x * (1 / 24 - x * (1 / 120 - x * (1 / 720)))))
        return weight * jnp.sqrt(x * series)

    def prepare(t):
        cols = lanes(t * wide, wide)
        rate = rates[:, cols]
        amp = amplitude(rate, weights[:, cols])
        for j, n in enumerate(nodes):
            coef[j : j + 1, cols] = jnp.sum(amp * jnp.exp(rate * (-float(n))), axis=0, keepdims=True)


    def owner_tables():
        mine = lanes(own * part, part)
        rate = rates[:, mine]
        amp = amplitude(rate, weights[:, mine])
        for j, n in enumerate(nodes):
            into[16 * j : 16 * j + 16, :] = jnp.exp(rate * (-float(CHUNK - 1 - n)))
            outof[16 * j : 16 * j + 16, :] = amp * jnp.exp(rate * (-float(1 + n)))
        sub = lax.broadcasted_iota(jnp.int32, (8, part), 0)
        far = (sub + 1).astype(F32) * (-float(CHUNK))
        for r in range(16):
            one = jnp.broadcast_to(rate[r : r + 1], (8, part))
            decay[r] = jnp.exp(one * far)
            for k, hop in enumerate((1, 2, 4)):
                decay_scan[3 * r + k] = jnp.where(sub >= hop, jnp.exp(one * (-float(CHUNK * hop))), 0.0)

    small[2].wait()
    small[3].wait()

    def lay(slot, start, edge):
        cols = lanes(start, 128)
        if edge:
            shifted[slot, 0:8, :] = jnp.where(ctx == 0, 0.0, halo[:, cols].astype(F32))
        for k in range(1 if edge == "only" else rows // 16):
            shifted[slot, 8 + 16 * k : 24 + 16 * k, :] = proj[16 * k : 16 * k + 16, cols].astype(F32)

    def tap_rows(start):
        cols = lanes(start, 128)
        block = taps[:, cols]
        return [jnp.broadcast_to(block[j : j + 1], (8, 128)) for j in range(taps.shape[0])]

    def filtered(slot, k, weights_j):
        total = None
        for j, w in enumerate(weights_j):
            term = shifted[slot, 8 + 8 * k - j : 16 + 8 * k - j, :] * w
            total = term if total is None else total + term
        return total

    def moment_copy(o):
        return pltpu.make_async_remote_copy(
            src_ref=send_m.at[o],
            dst_ref=recv_m.at[own],
            send_sem=m_send.at[o],
            recv_sem=m_recv.at[own],
            device_id={"ctx": base + o},
            device_id_type=MESH,
        )

    def moments(o):
        both = mm(gather[...], gated[:, lanes(o * part, part)])
        return (both[:16] + both[16:]).astype(BF16)

    def send_moments(o, value):
        send_m[o] = value

        @pl.when(o == own)
        def _():
            recv_m[own] = value

        @pl.when(o != own)
        def _():
            moment_copy(o).start()

    blocks = part // 128

    def edge_gate(o):
        for h in range(blocks):
            at = o * part + 128 * h
            lay(2 * blocks + 2 * h, width + at, "only")
            lay(2 * blocks + 2 * h + 1, 2 * width + at, "only")
            tk, tv = tap_rows(width + at), tap_rows(2 * width + at)
            both = filtered(2 * blocks + 2 * h, 0, tk) * filtered(2 * blocks + 2 * h + 1, 0, tv)
            gated[0:8, lanes(at, 128)] = both.astype(BF16)

    lag = 6
    per_quarter = quarter // part

    def gate(i, c):
        @pl.when(lax.rem(i, wide // part) == 0)
        def _():
            t = lax.div(i, wide // part)
            fetch(1, t).wait()
            fetch(2, t).wait()

        @pl.when(i == 3)
        def _():
            small[0].wait()
            small[1].wait()
            owner_tables()

        for n in range(4):
            if lag + n * per_quarter < GROUP:

                @pl.when(i == lag + n * per_quarter)
                def _(n=n):
                    halo_kv[2 * n].wait()
                    halo_kv[2 * n + 1].wait()

        @pl.when(i >= lag)
        def _():
            edge_gate(i - lag)
            send_moments(i - lag, moments(i - lag))

        for h in range(blocks):
            at = i * part + 128 * h
            lay(2 * h, width + at, None)
            lay(2 * h + 1, 2 * width + at, None)
            tk, tv = tap_rows(width + at), tap_rows(2 * width + at)
            for k in range(rows // 16):
                pair = [
                    filtered(2 * h, 2 * k + b, tk) * filtered(2 * h + 1, 2 * k + b, tv)
                    if k + b > 0
                    else jnp.zeros((8, 128), F32)
                    for b in range(2)
                ]
                gated[16 * k : 16 * k + 16, lanes(at, 128)] = jnp.concatenate(pair, 0).astype(BF16)
        return c

    lax.fori_loop(0, GROUP, gate, 0)

    for n in range(4):
        if lag + n * per_quarter >= GROUP:
            halo_kv[2 * n].wait()
            halo_kv[2 * n + 1].wait()
    for o in range(GROUP - lag, GROUP):
        edge_gate(o)
    for o in range(GROUP - lag, GROUP):
        send_moments(o, moments(o))
    small[4].wait()
    small[5].wait()
    halo_q.wait()

    def total_copy(x):
        return pltpu.make_async_remote_copy(
            src_ref=send_t,
            dst_ref=recv_t.at[row],
            send_sem=t_send.at[x],
            recv_sem=t_recv.at[row],
            device_id={"ctx": x * GROUP + own},
            device_id_type=MESH,
        )

    def total_arrival(x):
        return pltpu.make_async_remote_copy(
            src_ref=send_t,
            dst_ref=recv_t.at[x],
            send_sem=t_send.at[x],
            recv_sem=t_recv.at[x],
            device_id={"ctx": x * GROUP + own},
            device_id_type=MESH,
        )

    def moment_arrival(s):
        return pltpu.make_async_remote_copy(
            src_ref=send_m.at[s],
            dst_ref=recv_m.at[s],
            send_sem=m_send.at[s],
            recv_sem=m_recv.at[s],
            device_id={"ctx": base + s},
            device_id_type=MESH,
        )

    def past_copy(d):
        return pltpu.make_async_remote_copy(
            src_ref=send_g.at[d],
            dst_ref=recv_g.at[own],
            send_sem=g_send.at[d],
            recv_sem=g_recv.at[own],
            device_id={"ctx": base + d},
            device_id_type=MESH,
        )

    def past_arrival(s):
        return pltpu.make_async_remote_copy(
            src_ref=send_g.at[s],
            dst_ref=recv_g.at[s],
            send_sem=g_send.at[s],
            recv_sem=g_recv.at[s],
            device_id={"ctx": base + s},
            device_id_type=MESH,
        )

    halves = part // 128
    sub128 = lax.broadcasted_iota(jnp.int32, (8, 128), 0)

    def gather_states():
        def arrive(s, c):
            @pl.when(s != own)
            def _():
                moment_arrival(s).wait()

            return c

        lax.fori_loop(0, GROUP, arrive, 0)
        for s in range(GROUP):
            block = recv_m[s].astype(F32)
            for h in range(halves):
                plain_m[h, 16 * s : 16 * s + 16, :] = block[:, 128 * h : 128 * h + 128]

        for h in range(halves):
            cols = slice(128 * h, 128 * h + 128)

            def scan_group(g, c, h=h, cols=cols):
                m = [plain_m[h, pl.ds(g * 64 + j, 8, stride=8), :] for j in range(NODES)]
                for r in range(16):
                    state = None
                    for j in range(NODES):
                        term = m[j] * into[16 * j + r : 16 * j + r + 1, cols]
                        state = term if state is None else state + term
                    for k, hop in enumerate((1, 2, 4)):
                        state = state + decay_scan[3 * r + k, :, cols] * pltpu.roll(state, hop, 0)
                    scans[h, pl.ds(pl.multiple_of(r * 32 + 8 * g, 8), 8), :] = state
                return c

            lax.fori_loop(0, 4, scan_group, 0)
            step8 = jnp.exp(rates[:, lanes(own * part + 128 * h, 128)] * (-float(8 * CHUNK)))
            total = scans[h, pl.ds(7, 16, stride=32), :]
            for g in range(1, 4):
                total = total * step8 + scans[h, pl.ds(8 * g + 7, 16, stride=32), :]
            send_t[:, cols] = total

        def send(x, c):
            @pl.when(x != row)
            def _():
                total_copy(x).start()

            return c

        lax.fori_loop(0, outer, send, 0)

    def spread_states():
        def arrive(x, c):
            @pl.when(x != row)
            def _():
                total_arrival(x).wait()

            return c

        lax.fori_loop(0, outer, arrive, 0)
        for h in range(halves):
            cols = slice(128 * h, 128 * h + 128)
            rate = rates[:, lanes(own * part + 128 * h, 128)]
            step8 = jnp.exp(rate * (-float(8 * CHUNK)))
            step32 = jnp.exp(rate * (-float(32 * CHUNK)))
            held = jnp.zeros((16, 128), F32)
            for x in range(outer - 1):
                held = jnp.where(x < row, held * step32 + recv_t[x, :, cols], held)
            for g in range(4):
                carries[h, 16 * g : 16 * g + 16, :] = held
                held = held * step8 + scans[h, pl.ds(8 * g + 7, 16, stride=32), :]

        def spread_group(n, c):
            g = lax.rem(n + lax.div(own, 4), 4)
            for h in range(halves):
                cols = slice(128 * h, 128 * h + 128)
                states = []
                for r in range(16):
                    carry = jnp.broadcast_to(carries[h, pl.ds(16 * g + r, 1), :], (8, 128))
                    full = scans[h, pl.ds(pl.multiple_of(r * 32 + 8 * g, 8), 8), :] + decay[r, :, cols] * carry
                    states.append(jnp.where(sub128 == 0, carry, pltpu.roll(full, 1, 0)))
                for j in range(NODES):
                    past = None
                    for r in range(16):
                        term = states[r] * outof[16 * j + r : 16 * j + r + 1, cols]
                        past = term if past is None else past + term
                    plain_g[h, pl.ds(g * 64 + j, 8, stride=8), :] = past
                plain_g[h, pl.ds(g * 64 + NODES, 8, stride=8), :] = jnp.zeros((8, 128), F32)
            for b in range(4):
                d = 4 * g + b
                for h in range(halves):
                    block = plain_g[h, pl.ds(pl.multiple_of(16 * d, 16), 16), :]
                    send_g[d, :, 128 * h : 128 * h + 128] = block.astype(BF16)

            def send(b, c):
                d = 4 * g + lax.rem(b + own, 4)

                @pl.when(d == own)
                def _():
                    recv_g[own] = send_g[d]

                @pl.when(d != own)
                def _():
                    past_copy(d).start()

                return c

            lax.fori_loop(0, 4, send, 0)
            return c

        lax.fori_loop(0, 4, spread_group, 0)

    def within(t, c):
        fetch(0, t).wait()

        @pl.when(t == 0)
        def _():
            gather_states()

        @pl.when(t == 3)
        def _():
            spread_states()

        prepare(t)
        for piece in range(2):
            cols = lanes(t * wide + 256 * piece, 256)
            scale = coef[:, cols].astype(BF16)
            for half in range(2):
                tokens = slice(half * CHUNK, (half + 1) * CHUNK)
                field = gated[tokens, cols]
                stacked = jnp.concatenate([field * scale[j : j + 1] for j in range(NODES)], 0)
                result = mm(local[...], stacked)
                at = t * wide + 256 * piece + 128 * half
                slot = 2 * piece + half
                lay(slot, at, "all")
                tq = tap_rows(at)
                for k in range(rows // 8):
                    queries[8 * k : 8 * k + 8, lanes(at, 128)] = filtered(slot, k, tq)
                conv[tokens, cols] = result
        return c

    lax.fori_loop(0, steps, within, 0)

    def finish(t, c):
        per = wide // part
        for b in range(per):
            o = per * t + b

            @pl.when(o != own)
            def _(o=o):
                past_arrival(o).wait()

        for b in range(per):
            o = per * t + b
            cols = lanes(o * part, part)
            past = recv_g[o]
            past = jnp.concatenate([past, past], 0)
            for p in range(rows // CHUNK):
                tokens = slice(p * CHUNK, (p + 1) * CHUNK)
                result = mm(spread[tokens, :], past)
                queries[tokens, cols] = queries[tokens, cols] * (conv[tokens, cols] + result)
        return c

    lax.fori_loop(0, steps, finish, 0)


def shards(projected, taps, decays, residues):
    rows = projected.shape[0]
    width = taps.shape[1] // 3
    part = width // GROUP
    outer = lax.axis_size("ctx") // GROUP
    nodes, local, gather, spread = tables()
    turned = jnp.concatenate([decays, residues], 1).T
    hbm = pl.BlockSpec(memory_space=pltpu.HBM)
    dma = pltpu.SemaphoreType.DMA
    steps = width // 512
    return pl.pallas_call(
        functools.partial(kernel, nodes, width),
        out_shape=pltpu.VMEM((rows, width), F32),
        in_specs=[hbm] * 6,
        out_specs=pl.BlockSpec(memory_space=pltpu.VMEM),
        scratch_shapes=[
            pltpu.VMEM(taps.shape, F32),
            pltpu.VMEM((16, width), F32),
            pltpu.VMEM((16, width), F32),
            pltpu.VMEM(local.shape, BF16),
            pltpu.VMEM(gather.shape, BF16),
            pltpu.VMEM(spread.shape, BF16),
            pltpu.VMEM((rows, 3 * width), BF16),
            pltpu.VMEM((8, 3 * width), BF16),
            pltpu.VMEM((8, rows + 8, 128), F32),
            pltpu.VMEM((rows, width), BF16),
            pltpu.VMEM((rows, width), F32),
            pltpu.VMEM((8, width), F32),
            pltpu.VMEM((GROUP, 16, part), BF16),
            pltpu.VMEM((GROUP, 16, part), BF16),
            pltpu.VMEM((16, part), F32),
            pltpu.VMEM((outer, 16, part), F32),
            pltpu.VMEM((GROUP, 16, part), BF16),
            pltpu.VMEM((GROUP, 16, part), BF16),
            pltpu.VMEM((16 * NODES, part), F32),
            pltpu.VMEM((16 * NODES, part), F32),
            pltpu.VMEM((16, 8, part), F32),
            pltpu.VMEM((48, 8, part), F32),
            pltpu.VMEM((part // 128, 256, 128), F32),
            pltpu.VMEM((part // 128, 512, 128), F32),
            pltpu.VMEM((part // 128, 64, 128), F32),
            pltpu.VMEM((part // 128, 256, 128), F32),
            dma((6,)), dma((3, steps)),
            dma((9,)), dma((9,)),
            dma((GROUP,)), dma((GROUP,)),
            dma((outer,)), dma((outer,)),
            dma((GROUP,)), dma((GROUP,)),
        ],
        compiler_params=pltpu.CompilerParams(
            collective_id=0, has_side_effects=True, vmem_limit_bytes=60800 * 2**10
        ),
        name="hyena",
    )(projected, taps, turned, jnp.asarray(local), jnp.asarray(gather), jnp.asarray(spread))


def solution(mesh):
    in_specs = (P(("dp", "ctx"), None), P(), P(), P())
    out_specs = P(("dp", "ctx"), None)
    return jax.shard_map(shards, mesh=mesh, in_specs=in_specs, out_specs=out_specs, check_vma=False)
```
